32 devices in a mesh: mem: 2 (over core), rows: 16 (over z, y, x).
Axes of the slice: x: 2, y: 2, z: 4, core: 2. Of those that a mesh axis runs over, the one named last changes fastest.
Arguments:
- bin_index: int32 [15360, 32], P('rows', 'mem'), may hold values from 0 to 47
- labels: int32 [15360], P('rows'), may hold values from 0 to 7
- row_weight: float32 [15360], P('rows'), may hold values from 0.5 to 7.5
- bin_table: float32 [32, 48, 16], P('mem'), may hold values from -6 to 6
- table_first: float32 [32, 48, 16], P('mem'), may hold values from -2.670288e-05 to 2.670288e-05
- table_second: float32 [32, 48, 16], P('mem'), may hold values from 2.6490954e-13 to 1.0596382e-12
- weights: float32 [2, 512, 512], P('mem'), may hold values from -0.25 to 0.25
- weights_moment: float32 [2, 512, 512], P('mem'), may hold values from -0.0012207031 to 0.0012207031
- stat_left: float32 [2, 512, 512], P('mem'), may hold values from -2.6041667e-06 to 0.00026041667
- stat_right: float32 [2, 512, 512], P('mem'), may hold values from -2.6041667e-06 to 0.00026041667
- root_left: float32 [2, 512, 512], P('mem'), may hold values from -0.46952537 to 12.3948375
- root_right: float32 [2, 512, 512], P('mem'), may hold values from -0.46952537 to 12.3948375
- adapters: float32 [3, 2, 32, 512], P(None, None, 'mem'), may hold values from -1.2 to 1.4
- adapter_first: float32 [3, 2, 32, 512], P(None, None, 'mem'), may hold values from -6.1035156e-05 to 6.1035156e-05
- adapter_second: float32 [3, 2, 32, 512], P(None, None, 'mem'), may hold values from 1.6276042e-12 to 6.5104168e-12
- head_weight: float32 [32, 512, 8], P('mem'), may hold values from -0.25 to 0.25
- head_first: float32 [32, 512, 8], P('mem'), may hold values from -0.00024414062 to 0.00024414062
- head_second: float32 [32, 512, 8], P('mem'), may hold values from 2.6041667e-11 to 1.0416667e-10
- head_bias: float32 [32, 8], P('mem'), may hold values from -3 to 3
- bias_first: float32 [32, 8], P('mem'), may hold values from -0.00036621094 to 0.00036621094
- bias_second: float32 [32, 8], P('mem'), may hold values from 5.859375e-11 to 2.34375e-10
Outputs:
- loss_sum: float32 [], replicated
- var_sum: float32 [], replicated
- table_new: float32 [32, 48, 16], P('mem')
- table_first_new: float32 [32, 48, 16], P('mem')
- table_second_new: float32 [32, 48, 16], P('mem')
- weights_new: float32 [2, 512, 512], P('mem')
- moment_new: float32 [2, 512, 512], P('mem')
- left_new: float32 [2, 512, 512], P('mem')
- right_new: float32 [2, 512, 512], P('mem')
- adapters_new: float32 [3, 2, 32, 512], P(None, None, 'mem')
- adapter_first_new: float32 [3, 2, 32, 512], P(None, None, 'mem')
- adapter_second_new: float32 [3, 2, 32, 512], P(None, None, 'mem')
- head_new: float32 [32, 512, 8], P('mem')
- head_first_new: float32 [32, 512, 8], P('mem')
- head_second_new: float32 [32, 512, 8], P('mem')
- bias_new: float32 [32, 8], P('mem')
- bias_first_new: float32 [32, 8], P('mem')
- bias_second_new: float32 [32, 8], P('mem')
The draws below stay inside these ranges and needn't reach their ends.
All inputs are finite; a program needn't handle non-finite values.
Results may differ from the reference program's by a relative error of at most 0.0052.
Values may be sent and summed in bfloat16 or wider, within the bound.
A program may use at most 192 MiB of HBM per device.

```python
import math
import jax
import jax.numpy as jnp
from jax import lax

FEAT = 32
BINS = 48
EDIM = 16
WIDTH = 512
MEMBERS = 32
CLASSES = 8
LAYERS = 2
STEP = 10
ROWS_DEV = 960
TOTAL = 15360


def draw_row_weight(key, part):
    key = jax.random.fold_in(key, 3)
    position = jnp.arange(TOTAL, dtype=jnp.float32) / max(TOTAL - 1, 1)
    return (1.0 + 2.0 * position) * jax.random.uniform(key, (TOTAL,), jnp.float32, 0.7, 1.3)


def statistics_matrix(key):
    key_diag, key_rest = jax.random.split(key)
    diagonal = jnp.exp(jax.random.uniform(key_diag, (LAYERS, WIDTH), jnp.float32, 0.0, math.log(4.0))) / TOTAL
    rest = jnp.clip(jax.random.normal(key_rest, (LAYERS, WIDTH, WIDTH), jnp.float32), -4.0, 4.0) * (0.01 / TOTAL)
    rest = 0.5 * (rest + jnp.swapaxes(rest, 1, 2))
    identity = jnp.eye(WIDTH, dtype=jnp.float32)[None]
    return rest * (1.0 - identity) + diagonal[:, :, None] * identity


def root_matrix(key):
    key_diag, key_rest = jax.random.split(key)
    scale = (TOTAL / 2.5) ** 0.25
    diagonal = scale * jnp.exp(jax.random.uniform(key_diag, (LAYERS, WIDTH), jnp.float32, math.log(0.7), math.log(1.4)))
    rest = jnp.clip(jax.random.normal(key_rest, (LAYERS, WIDTH, WIDTH), jnp.float32), -4.0, 4.0) * (0.3 * scale / math.sqrt(WIDTH))
    rest = 0.5 * (rest + jnp.swapaxes(rest, 1, 2))
    identity = jnp.eye(WIDTH, dtype=jnp.float32)[None]
    return rest * (1.0 - identity) + diagonal[:, :, None] * identity


def draw_stat_left(key, part):
    key = jax.random.fold_in(key, 5)
    return statistics_matrix(key)


def draw_stat_right(key, part):
    key = jax.random.fold_in(key, 7)
    return statistics_matrix(key)


def draw_root_left(key, part):
    key = jax.random.fold_in(key, 11)
    return root_matrix(key)


def draw_root_right(key, part):
    key = jax.random.fold_in(key, 13)
    return root_matrix(key)


def draw_adapters(key, part):
    key = jax.random.fold_in(key, 17)
    key_scale, key_shift = jax.random.split(key)
    scales = jax.random.uniform(key_scale, (2, LAYERS, MEMBERS, WIDTH), jnp.float32, 0.6, 1.4)
    shifts = 0.3 * jnp.clip(jax.random.normal(key_shift, (1, LAYERS, MEMBERS, WIDTH), jnp.float32), -4.0, 4.0)
    return jnp.concatenate([scales, shifts], axis=0)


def place_ends(result, key, least, top_value):
    index_at = [jax.random.randint(jax.random.fold_in(key, axis), (), 0, length) for axis, length in enumerate(result.shape)]
    longest = result.shape.index(max(result.shape))
    neighbour = index_at[:longest] + [(index_at[longest] + 1) % result.shape[longest]] + index_at[longest + 1:]
    return result.at[tuple(index_at)].set(least).at[tuple(neighbour)].set(top_value)


def levels(own_key, shape, pieces, low, top_value):
    loudness = 1.0
    for dim, parts in pieces:
        draws = jax.random.uniform(jax.random.fold_in(jax.random.fold_in(own_key, 6), dim), (parts,), jnp.float32, low / len(pieces), top_value / len(pieces))
        loudness = loudness * jnp.repeat(jnp.exp(draws), shape[dim] // parts).reshape((-1,) + (1,) * (len(shape) - 1 - dim))
    return loudness


def normal_values(key, extent, scale, most, shards=(), kind=jnp.bfloat16):
    loudness = levels(key, extent, shards, -0.22, 0.18) if shards else 1.0
    drawn = jax.random.normal(key, extent, jnp.float32) * scale * loudness
    return jnp.minimum(jnp.maximum(drawn, -most), most).astype(kind)


def setup_inputs(seed: int = 0) -> dict:
    key_list = jax.random.split(jax.random.key(seed), 22)
    bin_index = place_ends(jax.random.randint(key_list[0], (TOTAL, FEAT), 0, BINS), jax.random.fold_in(key_list[0], 1), 0, BINS - 1).astype(jnp.int32)
    labels = place_ends(jax.random.randint(key_list[1], (TOTAL,), 0, CLASSES), jax.random.fold_in(key_list[1], 1), 0, CLASSES - 1).astype(jnp.int32)
    row_weight = draw_row_weight(jax.random.fold_in(key_list[21], 71), 0)
    bin_table = normal_values(key_list[3], (FEAT, BINS, EDIM), 1.0, 6.0, ((0, 2),), jnp.float32)
    table_first = normal_values(key_list[4], (FEAT, BINS, EDIM), (0.011 / (BINS * (MEMBERS * WIDTH) ** 0.5)), 2.6702880859375e-05, ((0, 2),), jnp.float32)
    table_second = jnp.clip(jnp.exp(math.log(1.059638162805021e-12) - 1.3862944 * jax.random.uniform(key_list[5], (FEAT, BINS, EDIM), jnp.float32) ** levels(key_list[5], (FEAT, BINS, EDIM), ((0, 2),), -0.2, 0.2)), 2.649095407012553e-13, 1.059638162805021e-12)
    weights = normal_values(key_list[6], (LAYERS, WIDTH, WIDTH), WIDTH ** -0.5, 0.25, ((0, 2),), jnp.float32)
    weights_moment = normal_values(key_list[7], (LAYERS, WIDTH, WIDTH), (0.01 / TOTAL ** 0.5), 0.0012207031, ((0, 2),), jnp.float32)
    stat_left = draw_stat_left(jax.random.fold_in(key_list[21], 71), 0)
    stat_right = draw_stat_right(jax.random.fold_in(key_list[21], 71), 0)
    root_left = draw_root_left(jax.random.fold_in(key_list[21], 71), 0)
    root_right = draw_root_right(jax.random.fold_in(key_list[21], 71), 0)
    adapters = draw_adapters(jax.random.fold_in(key_list[21], 71), 0)
    adapter_first = normal_values(key_list[13], (3, LAYERS, MEMBERS, WIDTH), (0.00055 / TOTAL ** 0.5), 6.103515625e-05, ((2, 2),), jnp.float32)
    adapter_second = jnp.clip(jnp.exp(math.log(6.510416771660088e-12) - 1.3862944 * jax.random.uniform(key_list[14], (3, LAYERS, MEMBERS, WIDTH), jnp.float32) ** levels(key_list[14], (3, LAYERS, MEMBERS, WIDTH), ((2, 2),), -0.2, 0.2)), 1.627604192915022e-12, 6.510416771660088e-12)
    head_weight = normal_values(key_list[15], (MEMBERS, WIDTH, CLASSES), WIDTH ** -0.5, 0.25, ((0, 2),), jnp.float32)
    head_first = normal_values(key_list[16], (MEMBERS, WIDTH, CLASSES), (0.0022 / TOTAL ** 0.5), 0.00024414062, ((0, 2),), jnp.float32)
    head_second = jnp.clip(jnp.exp(math.log(1.0416666834656141e-10) - 1.3862944 * jax.random.uniform(key_list[17], (MEMBERS, WIDTH, CLASSES), jnp.float32) ** levels(key_list[17], (MEMBERS, WIDTH, CLASSES), ((0, 2),), -0.2, 0.2)), 2.6041667086640352e-11, 1.0416666834656141e-10)
    head_bias = normal_values(key_list[18], (MEMBERS, CLASSES), 0.5, 3.0, ((0, 2),), jnp.float32)
    bias_first = normal_values(key_list[19], (MEMBERS, CLASSES), (0.0033 / TOTAL ** 0.5), 0.00036621094, ((0, 2),), jnp.float32)
    bias_second = jnp.clip(jnp.exp(math.log(2.3437499163669884e-10) - 1.3862944 * jax.random.uniform(key_list[20], (MEMBERS, CLASSES), jnp.float32) ** levels(key_list[20], (MEMBERS, CLASSES), ((0, 2),), -0.2, 0.2)), 5.859374790917471e-11, 2.3437499163669884e-10)
    return dict(bin_index=bin_index, labels=labels, row_weight=row_weight, bin_table=bin_table, table_first=table_first, table_second=table_second, weights=weights, weights_moment=weights_moment, stat_left=stat_left, stat_right=stat_right, root_left=root_left, root_right=root_right, adapters=adapters, adapter_first=adapter_first, adapter_second=adapter_second, head_weight=head_weight, head_first=head_first, head_second=head_second, head_bias=head_bias, bias_first=bias_first, bias_second=bias_second)


PRECISE = lax.Precision.HIGHEST
LR_TABLE = 1.0
LR_ADAPTER = 0.7
LR_HEAD = 0.15
LR_BIAS = 0.5
LR_SHAMPOO = 4.0
DECAY_FIRST = 0.9
DECAY_SECOND = 0.999
DECAY_STAT = 0.95
MOMENTUM = 0.9
WEIGHT_DECAY = 0.01
EPSILON = 1e-08

@jax.custom_vjp
def low(v):
    return lax.optimization_barrier(v.astype(jnp.bfloat16)).astype(jnp.float32)

@jax.custom_vjp
def low_back(v):
    return v

def low_keep(v):
    return (low(v), None)

def low_pass(kept, grad):
    return (grad,)

def back_keep(v):
    return (v, None)

def back_low(kept, grad):
    return (low(grad),)
low.defvjp(low_keep, low_pass)
low_back.defvjp(back_keep, back_low)

def forward_block(params, block_bins, block_labels, block_weight):
    bin_table, weights, adapters, head_weight, head_bias = params
    feature_ids = jnp.arange(FEAT, dtype=jnp.int32)[None, :]
    looked = bin_table[feature_ids, block_bins]
    inputs = low(looked.reshape(block_bins.shape[0], WIDTH))[None]
    for layer_no in range(LAYERS):
        products = low(inputs * adapters[0, layer_no][:, None, :])
        zvalue = low_back(jnp.einsum('mnw,wv->mnv', products, low(weights[layer_no]), precision=PRECISE))
        inputs = jax.nn.silu(zvalue * adapters[1, layer_no][:, None, :] + adapters[2, layer_no][:, None, :])
    logits = low_back(jnp.einsum('mnw,mwc->mnc', low(inputs), low(head_weight), precision=PRECISE)) + head_bias[:, None, :]
    member_prob = jax.nn.softmax(logits, axis=-1)
    mean_prob = lax.optimization_barrier(jnp.mean(member_prob, axis=0))
    target = (block_labels[:, None] == jnp.arange(CLASSES, dtype=jnp.int32)[None, :]).astype(jnp.float32)
    picked = lax.optimization_barrier(jnp.sum(mean_prob * target, axis=-1))
    weighted = block_weight * -jnp.log(picked)
    spread = lax.optimization_barrier(jnp.mean(lax.optimization_barrier(jnp.sum((member_prob - mean_prob[None]) ** 2, axis=-1)), axis=0))
    return (jnp.sum(weighted) / TOTAL, (jnp.sum(weighted), jnp.sum(block_weight * spread)))

def adamw_update(value, grad, first, second, rate):
    first_new = DECAY_FIRST * first + (1.0 - DECAY_FIRST) * grad
    second_new = DECAY_SECOND * second + (1.0 - DECAY_SECOND) * grad * grad
    first_hat = first_new / (1.0 - DECAY_FIRST ** STEP)
    second_hat = second_new / (1.0 - DECAY_SECOND ** STEP)
    value_new = value - rate * (first_hat / (jnp.sqrt(second_hat) + EPSILON) + WEIGHT_DECAY * value)
    return (value_new, first_new, second_new)

def shampoo_update(grad, weights, moment, stat_left, stat_right, root_left, root_right):
    moment_new = MOMENTUM * moment + grad
    direction = jnp.matmul(jnp.matmul(root_left, moment_new, precision=PRECISE), root_right, precision=PRECISE)
    weights_new = weights - LR_SHAMPOO * direction
    flipped = jnp.swapaxes(grad, 1, 2)
    left_new = DECAY_STAT * stat_left + jnp.matmul(grad, flipped, precision=PRECISE)
    right_new = DECAY_STAT * stat_right + jnp.matmul(flipped, grad, precision=PRECISE)
    return (weights_new, moment_new, left_new, right_new)

def reference(bin_index, labels, row_weight, bin_table, table_first, table_second, weights, weights_moment, stat_left, stat_right, root_left, root_right, adapters, adapter_first, adapter_second, head_weight, head_first, head_second, head_bias, bias_first, bias_second):
    params = (bin_table, weights, adapters, head_weight, head_bias)
    blocks = TOTAL // ROWS_DEV
    batch = (bin_index.reshape(blocks, ROWS_DEV, FEAT), labels.reshape(blocks, ROWS_DEV), row_weight.reshape(blocks, ROWS_DEV))

    def objective(values):
        checked = jax.checkpoint(forward_block)

        def block_step(carry, block):
            loss, extra = checked(values, block[0], block[1], block[2])
            return ((carry[0] + loss, carry[1] + extra[0], carry[2] + extra[1]), None)
        zero = jnp.zeros((), jnp.float32)
        totals, _ = lax.scan(block_step, (zero, zero, zero), batch)
        return (totals[0], (totals[1], totals[2]))
    loss, pullback, sums = jax.vjp(objective, params, has_aux=True)
    grads = pullback(jnp.ones_like(loss))[0]
    grad_table, grad_weights, grad_adapters, grad_head, grad_bias = grads
    table_new, table_first_new, table_second_new = adamw_update(bin_table, grad_table, table_first, table_second, LR_TABLE)
    adapters_new, adapter_first_new, adapter_second_new = adamw_update(adapters, grad_adapters, adapter_first, adapter_second, LR_ADAPTER)
    head_new, head_first_new, head_second_new = adamw_update(head_weight, grad_head, head_first, head_second, LR_HEAD)
    bias_new, bias_first_new, bias_second_new = adamw_update(head_bias, grad_bias, bias_first, bias_second, LR_BIAS)
    weights_new, moment_new, left_new, right_new = shampoo_update(grad_weights, weights, weights_moment, stat_left, stat_right, root_left, root_right)
    return (sums[0], sums[1], table_new, table_first_new, table_second_new, weights_new, moment_new, left_new, right_new, adapters_new, adapter_first_new, adapter_second_new, head_new, head_first_new, head_second_new, bias_new, bias_first_new, bias_second_new)
```

```python
import functools

import jax
import jax.numpy as jnp
from jax import lax
from jax.experimental import pallas as pl
from jax.experimental.pallas import tpu as pltpu
from jax.sharding import PartitionSpec as P

STEP = 10
LR_TABLE = 1.0
LR_ADAPTER = 0.7
LR_HEAD = 0.15
LR_BIAS = 0.5
LR_SHAMPOO = 4.0
DECAY_FIRST = 0.9
DECAY_SECOND = 0.999
DECAY_STAT = 0.95
MOMENTUM = 0.9
WEIGHT_DECAY = 0.01
EPSILON = 1e-08

F32 = jnp.float32
BF16 = jnp.bfloat16
MESH = pl.DeviceIdType.MESH
LANES = 128
TILE = 16
SHARES = 16
INNER = 4


def contract(a, b, a_dim, b_dim):
    return lax.dot_general(
        a, b, (((a_dim,), (b_dim,)), ((), ())), preferred_element_type=F32
    )


def column(row):
    return jnp.broadcast_to(row, (LANES, row.shape[1])).T


def member_matrix(matrix, in_column, out_row):
    parts = []
    for start in range(0, matrix.shape[1], LANES):
        cols = slice(start, start + LANES)
        parts.append((matrix[:, cols].astype(F32) * in_column * out_row[:, cols]).astype(BF16))
    return jnp.concatenate(parts, axis=1)


def slope(rise, active):
    return rise + active * (2.0 - rise)


def spread_product(product, matrix, in_column, half_row, total):
    row_sum = None
    out_grads = []
    for start in range(0, matrix.shape[1], LANES):
        cols = slice(start, start + LANES)
        part = product[:, cols]
        scale = half_row[:, cols]
        mixed = matrix[:, cols] * part
        total[:, cols] += in_column * part * scale
        out_grads.append(jnp.sum(in_column * mixed, axis=0, keepdims=True))
        mixed = mixed * scale
        row_sum = mixed if row_sum is None else row_sum + mixed
    return row_sum, 0.5 * jnp.concatenate(out_grads, axis=1)


def row_of(sums):
    return jnp.sum(sums.T, axis=0, keepdims=True)


def run_units(units):
    ready = units[0][0]()
    result = units[0][1](ready)
    ready = units[1][0]() if len(units) > 1 else None
    for k, (_, _, finish) in enumerate(units):
        following = None
        if k + 1 < len(units):
            following = units[k + 1][1](ready)
            if k + 2 < len(units):
                ready = units[k + 2][0]()
        finish(result)
        result = following


def once(function):
    held = []

    def get():
        if not held:
            held.append(function())
        return held[0]

    return get


def nothing(*_):
    return None


class Exchange:
    def __init__(self, sems, first_sem, n_rows, inner, buf, near, mid, far, done, out, base, core):
        self.sems, self.first = sems, first_sem
        self.inner, self.outer = inner, n_rows // inner
        self.buf, self.near, self.mid, self.far, self.done = buf, near, mid, far, done
        self.out, self.base, self.core = out, base, core
        self.tiles = buf.shape[0]
        self.per = self.tiles // n_rows
        self.block = self.per * self.outer
        self.mem = lax.axis_index("mem")
        self.me = lax.axis_index("rows")
        self.my_in = lax.rem(self.me, inner)
        self.my_out = self.me // inner
        self.here = (self.my_in * self.outer + self.my_out) * self.per

    def send(self, src, dst, sem, core, peer):
        pltpu.make_async_remote_copy(
            src_ref=src,
            dst_ref=dst,
            send_sem=self.sems.at[self.first + 2 * sem],
            recv_sem=self.sems.at[self.first + 2 * sem + 1],
            device_id=(core, peer),
            device_id_type=MESH,
        ).start()

    def wait(self, tiles, sem, received):
        src = self.buf if self.inner == 1 else self.mid
        part = (self.buf, src, self.done, self.out)[sem].at[pl.ds(0, tiles)]
        pltpu.make_async_copy(part, part, self.sems.at[self.first + 2 * sem + received]).wait()

    def each_near(self, step):
        def body(k, carry):
            peer = lax.rem(self.my_in + k, self.inner)
            step(k, peer, self.my_out * self.inner + peer)
            return carry

        lax.fori_loop(1, self.inner, body, 0)

    def each_far(self, step):
        def body(k, carry):
            peer = lax.rem(self.my_out + k, self.outer)
            step(k, peer, peer * self.inner + self.my_in)
            return carry

        lax.fori_loop(1, self.outer, body, 0)

    def start(self):
        if self.inner == 1:
            self.send_far(self.buf)
        else:
            self.each_near(
                lambda k, peer, device: self.send(
                    self.buf.at[pl.ds(peer * self.block, self.block)],
                    self.near.at[k - 1],
                    0,
                    self.mem,
                    device,
                )
            )

    def add_near(self):
        self.wait((self.inner - 1) * self.block, 0, 1)
        total = self.buf[pl.ds(self.my_in * self.block, self.block)].astype(F32)
        for k in range(self.inner - 1):
            total = total + self.near[k].astype(F32)
        self.mid[...] = total.astype(self.mid.dtype)
        self.send_far(self.mid)

    def send_far(self, src):
        self.each_far(
            lambda k, peer, device: self.send(
                src.at[pl.ds(peer * self.per, self.per)], self.far.at[k - 1], 1, self.mem, device
            )
        )

    def add_far(self):
        src = self.buf if self.inner == 1 else self.mid
        self.wait((self.outer - 1) * self.per, 1, 1)

        def body(k, total):
            return total + self.far[k].astype(F32)

        own = src[pl.ds(self.my_out * self.per, self.per)].astype(F32)
        total = lax.fori_loop(0, self.outer - 1, body, own)
        part = pl.ds(self.here, self.per)
        self.done[part] = total.astype(self.done.dtype)
        if self.inner == 1:
            self.hand_out(self.here, self.per, self.each_far)
        else:
            self.each_far(
                lambda k, peer, device: self.send(
                    self.done.at[part], self.done.at[part], 2, self.mem, device
                )
            )

    def spread(self):
        self.wait((self.outer - 1) * self.per, 2, 1)
        self.hand_out(self.my_in * self.block, self.block, self.each_near)

    def hand_out(self, at, size, each):
        src = self.done.at[pl.ds(at, size)]
        if self.core is None:
            dst = self.out.at[pl.ds(self.base + at, size)]
            each(lambda k, peer, device: self.send(src, dst, 3, self.mem, device))
            dst[...] = src[...]
        else:
            dst = self.out.at[pl.ds(self.base + self.mem * self.tiles + at, size)]
            each(lambda k, peer, device: self.send(src, dst, 3, self.core, device))

            @pl.when(self.mem == self.core)
            def _():
                dst[...] = src[...]

            @pl.when(self.mem != self.core)
            def _():
                self.send(src, dst, 3, self.core, self.me)

    def finish(self):
        if self.inner > 1:
            self.wait((self.inner - 1) * self.block, 0, 0)
            self.wait((self.outer - 1) * self.per, 2, 0)
            own, peers = self.block, self.inner - 1
        else:
            own, peers = self.per, self.outer - 1
        self.wait((self.outer - 1) * self.per, 1, 0)
        if self.core is None:
            self.wait(self.tiles - own, 3, 1)
            self.wait(peers * own, 3, 0)
        else:

            @pl.when(self.mem == self.core)
            def _():
                self.wait(2 * self.tiles - own, 3, 1)
                self.wait(peers * own, 3, 0)

            @pl.when(self.mem != self.core)
            def _():
                self.wait((peers + 1) * own, 3, 0)


EXCHANGE_SEMS = 10


class Handover(Exchange):
    def __init__(self, buf, out, base):
        self.buf, self.out, self.base = buf, out, base

    def start(self):
        self.out[pl.ds(self.base, self.buf.shape[0])] = self.buf[...].astype(self.out.dtype)

    def add_near(self):
        pass

    add_far = spread = finish = add_near


SLOTS = 4


def step_kernel(
    n_rows,
    inner,
    bins_ref,
    label_ref,
    weight_ref,
    table_ref,
    matrix_ref,
    adapt_ref,
    head_ref,
    bias_ref,
    wide_out,
    second_out,
    first_out,
    table_out,
    misc_out,
    act2,
    rise1,
    embed,
    mats,
    mats_t,
    keep1,
    act1,
    prob,
    slots,
    rises,
    embed_t,
    stage_w,
    stage_e,
    grad_e,
    grad_w,
    sums,
    spreads,
    pair_e,
    pair_w,
    wide_rows,
    head_grads,
    misc,
    sems,
    slot_sems,
    *stages,
):
    mem = lax.axis_index("mem")
    me = lax.axis_index("rows")
    other = 1 - mem
    rows, width = embed.shape
    members, classes = head_ref.shape[0], head_ref.shape[1]
    own_feat, edim, bins = table_ref.shape
    own_cols = own_feat * edim
    total_rows = rows * n_rows
    total_members = 2 * members
    half_rows = half_cols = width // 2
    across = width // LANES
    halves = [slice(0, half_cols), slice(half_cols, width)]
    my_cols = pl.ds(pl.multiple_of(mem * own_cols, own_cols), own_cols)
    their_cols = pl.ds(pl.multiple_of(other * own_cols, own_cols), own_cols)
    their_half = pl.ds(pl.multiple_of(other * half_rows, half_rows), half_rows)
    my_half = pl.ds(pl.multiple_of(mem * half_rows, half_rows), half_rows)

    barrier = pltpu.get_barrier_semaphore()
    line = me * 2 + mem

    def greet(k, carry):
        peer = lax.rem(line + k, 2 * n_rows)
        pl.semaphore_signal(
            barrier, inc=1, device_id=(lax.rem(peer, 2), peer // 2), device_id_type=MESH
        )
        return carry

    lax.fori_loop(1, 2 * n_rows, greet, 0)

    def to_partner(src, dst, sem):
        return pltpu.make_async_remote_copy(
            src_ref=src,
            dst_ref=dst,
            send_sem=sems.at[sem],
            recv_sem=sems.at[sem + 1],
            device_id=(other, me),
            device_id_type=MESH,
        )

    def adapter(kind, layer, m, cols=slice(None)):
        return adapt_ref[kind, layer, pl.ds(m, 1), cols]

    def one_hot():
        parts = []
        for f in range(own_feat):
            ids = lax.broadcasted_iota(jnp.int32, (bins, rows), 0)
            parts.append((bins_ref[f : f + 1, :] == ids).astype(F32))
        return jnp.concatenate(parts, axis=0).astype(BF16)

    blocks = []
    for f in range(own_feat):
        pads = [table_ref[f]]
        if f > 0:
            pads.insert(0, jnp.zeros((edim, bins * f), F32))
        if f < own_feat - 1:
            pads.append(jnp.zeros((edim, bins * (own_feat - 1 - f)), F32))
        blocks.append(jnp.concatenate(pads, axis=1))
    lookup = jnp.concatenate(blocks, axis=0).astype(BF16)
    embed[:, my_cols] = contract(lookup, one_hot(), 1, 0).T.astype(BF16)
    own_low = matrix_ref[...].astype(BF16)
    outgoing = stage_w.at[pl.ds(0, width), :]
    outgoing[...] = own_low
    mats[mem] = own_low.astype(F32)

    pl.semaphore_wait(barrier, 2 * n_rows - 1)
    copy_e = to_partner(embed.at[:, my_cols], embed.at[:, my_cols], 0)
    copy_w = to_partner(outgoing, pair_w.at[pl.ds(0, width), :], 2)
    copy_e.start()
    copy_w.start()
    copy_w.wait()
    mats[other] = pair_w[0:width, :].astype(F32)
    copy_e.wait()

    def scaled(layer, m, col, cols):
        return member_matrix(mats[layer, :, cols], col(), 0.5 * adapter(1, layer, m, cols))

    def first_units(m, slot):
        col = once(lambda: column(adapter(0, 0, m)))

        def unit(cols):
            def finish(product):
                half = product + 0.5 * adapter(2, 0, m, cols)
                rise = 1.0 + jnp.tanh(half)
                act1[m, :, cols] = (half * rise).astype(BF16)
                rises[slot, :, cols] = rise.astype(BF16)

            return (
                lambda: scaled(0, m, col, cols),
                lambda low: contract(embed[...], low, 1, 0),
                finish,
            )

        return [unit(cols) for cols in halves]

    def second_units(m, slot):
        col = once(lambda: column(adapter(0, 1, m)))

        def unit(cols):
            def finish(product):
                half = product + 0.5 * adapter(2, 1, m, cols)
                rise = 1.0 + jnp.tanh(half)
                slots[slot, :, cols] = (half * rise).astype(BF16)
                keep1[m, :, cols] = rise.astype(BF16)

            return (
                lambda: scaled(1, m, col, cols),
                lambda low: contract(act1[m], low, 1, 0),
                finish,
            )

        return [unit(cols) for cols in halves]

    def head_unit(m, slot):

        def finish(logits):
            lane = lax.broadcasted_iota(jnp.int32, (classes, members), 1)
            shift = jnp.sum(jnp.where(lane == m, bias_ref[...], 0.0), axis=1, keepdims=True)
            logits = logits + shift
            power = jnp.exp(logits - jnp.max(logits, axis=0, keepdims=True))
            share = power / jnp.sum(power, axis=0, keepdims=True)
            prob[m] = share
            sums[0] += share

        return (nothing, lambda _: contract(head_ref[m].astype(BF16), slots[slot], 1, 1), finish)

    def slot_copy(m, outward):
        slot = lax.rem(m, SLOTS)
        src, dst = slots.at[slot], act2.at[m]
        if not outward:
            src, dst = dst, src
        return pltpu.make_async_copy(src, dst, slot_sems.at[slot])

    def rise_copy(m, outward):
        slot = lax.rem(m + SLOTS - 1, SLOTS)
        src, dst = rises.at[slot], rise1.at[m]
        if not outward:
            src, dst = dst, src
        return pltpu.make_async_copy(src, dst, slot_sems.at[SLOTS + slot])

    sums[0] = jnp.zeros((classes, rows), F32)
    run_units(first_units(0, SLOTS - 1))
    rise_copy(0, True).start()

    def forward(m, slot, with_next):
        run_units(
            second_units(m, slot)
            + first_units(m + 1, slot)
            + [head_unit(m, slot)]
            + second_units(m + 1, slot + 1)
            + (first_units(m + 2, slot + 1) if with_next else [(nothing,) * 3])
            + [head_unit(m + 1, slot + 1)]
        )
        slot_copy(m, True).start()
        slot_copy(m + 1, True).start()
        rise_copy(m + 1, True).start()
        if with_next:
            rise_copy(m + 2, True).start()

    def forward_step(i, carry):
        m = 2 * i

        @pl.when(i >= 1)
        def _():
            rise_copy(m - 2, True).wait()

        @pl.when(i >= 2)
        def _():
            rise_copy(m - 3, True).wait()
            slot_copy(m - 4, True).wait()
            slot_copy(m - 3, True).wait()

        forward(m, 2 * lax.rem(i, 2), True)
        return carry

    lax.fori_loop(0, members // 2 - 1, forward_step, 0)
    rise_copy(members - 4, True).wait()
    rise_copy(members - 5, True).wait()
    slot_copy(members - 6, True).wait()
    slot_copy(members - 5, True).wait()
    forward(members - 2, (members - 2) % SLOTS, False)
    copy_p = to_partner(sums.at[0], sums.at[1], 4)
    copy_p.start()
    for m in range(members - 4, members):
        slot_copy(m, True).wait()
    for m in range(members - 3, members):
        rise_copy(m, True).wait()
    for m in range(3):
        slot_copy(m, False).start()
    for m in range(SLOTS):
        rise_copy(m, False).start()
    embed_t[...] = jnp.zeros_like(embed_t)
    embed_t[:, 0:rows] = embed[...].T
    for layer in range(2):
        mats_t[layer] = mats[layer].T.astype(BF16)
    grad_w[...] = jnp.zeros_like(grad_w)
    grad_e[...] = jnp.zeros_like(grad_e)
    copy_p.wait()
    mean = (sums[0] + sums[1]) * (1.0 / total_members)
    target = (
        label_ref[...] == lax.broadcasted_iota(jnp.int32, (classes, rows), 0)
    ).astype(F32)
    picked = jnp.sum(mean * target, axis=0, keepdims=True)
    row_weight = weight_ref[...]
    factor = row_weight / (total_rows * total_members * picked)
    loss = jnp.sum(row_weight * -jnp.log(picked), axis=1, keepdims=True)

    def deviation(m, total):
        gap = prob[m] - mean
        return total + jnp.sum(gap * gap, axis=0, keepdims=True)

    spreads[0, 0:1] = lax.fori_loop(0, members, deviation, jnp.zeros((1, rows), F32))
    copy_s = to_partner(spreads.at[0], spreads.at[1], 6)
    copy_s.start()
    misc[...] = jnp.zeros_like(misc)
    spot = lax.broadcasted_iota(jnp.int32, (classes, LANES), 1)

    def logit_units(m):
        slot = lax.rem(m, SLOTS)

        @once
        def grads():
            share = prob[m]
            own_pick = jnp.sum(share * target, axis=0, keepdims=True)
            grad = -(factor * own_pick) * (target - share)
            return grad.astype(BF16), grad.T.astype(BF16), jnp.sum(grad, axis=1, keepdims=True)

        def unit(cols):
            def finish(product):
                grad = product.astype(BF16) * slope(keep1[m, :, cols], slots[slot, :, cols])
                wide_rows[2, 1, pl.ds(m, 1), cols] = 0.5 * jnp.sum(
                    grad.astype(F32), axis=0, keepdims=True
                )
                keep1[m, :, cols] = grad

            return (
                nothing,
                lambda _: contract(grads()[1], head_ref[m, :, cols].astype(BF16), 1, 0),
                finish,
            )

        def finish(product):
            head_grads[m] = product
            misc[...] = jnp.where(spot == m, grads()[2], misc[...])

        return [unit(cols) for cols in halves] + [
            (nothing, lambda _: contract(grads()[0], slots[slot], 1, 0), finish)
        ]

    def product_units(m):
        col = once(lambda: column(adapter(0, 1, m)))
        turned = once(lambda: act1[m].T)
        kept = []

        def unit(cols):
            def finish(product):
                row_sum, out_grad = spread_product(
                    product, mats[1, :, cols], col(), 0.5 * adapter(1, 1, m, cols), grad_w.at[:, cols]
                )
                wide_rows[1, 1, pl.ds(m, 1), cols] = out_grad
                kept.append(row_sum)
                if len(kept) == len(halves):
                    wide_rows[0, 1, pl.ds(m, 1), :] = row_of(kept[0] + kept[1])

            return turned, lambda low: contract(low, keep1[m, :, cols], 1, 0), finish

        return [unit(cols) for cols in halves]

    slot_copy(0, False).wait()
    run_units(logit_units(0))

    def back_second(m, with_next):
        def mixed(m, with_next):
            left, right = product_units(m)
            if not with_next:
                return [left, right]
            first, second, head = logit_units(m + 1)
            return [left, first, right, second, head]

        run_units(mixed(m, True) + mixed(m + 1, with_next))

    def back_second_step(i, carry):
        m = 2 * i
        slot_copy(m + 1, False).wait()
        slot_copy(m + 2, False).wait()
        slot_copy(m + 3, False).start()

        @pl.when(i < members // 2 - 2)
        def _():
            slot_copy(m + 4, False).start()

        back_second(m, True)
        return carry

    lax.fori_loop(0, members // 2 - 1, back_second_step, 0)
    slot_copy(members - 1, False).wait()
    back_second(members - 2, False)

    def put(buf, first_tile, block):
        down, broad = block.shape[0] // TILE, block.shape[1] // LANES
        for i in range(down):
            for j in range(broad):
                buf[first_tile + i * broad + j] = block[
                    i * TILE : (i + 1) * TILE, j * LANES : (j + 1) * LANES
                ].astype(BF16)

    def clear(buf, first_tile):
        for t in range(first_tile, buf.shape[0]):
            buf[t] = jnp.zeros((TILE, LANES), BF16)

    half_tiles = half_rows // TILE * across
    plan = (
        (inner, wide_out, 0, half_tiles, 1),
        (inner, second_out, 0, 0, None),
        (1, table_out, 0, 0, None),
        (1, wide_out, 0, 0, 0),
        (1, wide_out, half_tiles, half_tiles // 2, 0),
        (1, first_out, 0, 0, None),
    )
    exchanges = []
    for i, (near, out, base, own_base, core) in enumerate(plan):
        refs = stages[5 * i : 5 * i + 5]
        if inner:
            first_sem = 16 + EXCHANGE_SEMS * i
            exchanges.append(Exchange(sems, first_sem, n_rows, near, *refs, out, base, core))
        else:
            exchanges.append(Handover(refs[0], out, own_base))
    second_w, second_s, table_x, block0_x, block1_x, first_x = exchanges

    def send_half(slot, cols):
        broad = cols.stop - cols.start
        src = stage_w.at[pl.ds(half_rows * slot, half_rows), pl.ds(0, broad)]
        src[...] = grad_w[their_half, cols].astype(BF16)
        dst = pair_w.at[pl.ds(half_rows * slot, half_rows), pl.ds(0, broad)]
        copy = to_partner(src, dst, 8 + 2 * slot)
        copy.start()

        def take():
            copy.wait()
            return grad_w[my_half, cols] + dst[...].astype(F32)

        return take

    take_second = send_half(0, slice(0, width))

    def begin_second_small():
        place = 0
        for m in range(0, members, 2):
            put(second_s.buf, place, jnp.concatenate([head_grads[m], head_grads[m + 1]], axis=0))
            place += across
        for i in range(3):
            put(second_s.buf, place, wide_rows[i, 1])
            place += across
        clear(second_s.buf, place)
        second_s.start()
        copy_s.wait()
        spread = (spreads[0, 0:1] + spreads[1, 0:1]) * (1.0 / total_members)
        variance = jnp.sum(row_weight * spread, axis=1, keepdims=True)
        misc[...] = jnp.where(
            spot == members, loss, jnp.where(spot == members + 1, variance, misc[...])
        )
        if inner:

            def tell(k, carry):
                second_s.send(misc, misc_out.at[me], 4, mem, lax.rem(me + k, n_rows))
                return carry

            lax.fori_loop(1, n_rows, tell, 0)
            misc_out[me] = misc[...]
        else:
            misc_out[0] = misc[...]

    def begin_second_wide():
        put(second_w.buf, 0, take_second())
        second_w.start()
        grad_w[...] = jnp.zeros_like(grad_w)

    def at(m, steps):
        for when, step in steps:
            pl.when(m == when)(step)

    def each(name, *exchanges):
        def step():
            for exchange in exchanges:
                getattr(exchange, name)()

        return step

    def back_units(m):
        col = once(lambda: column(0.5 * adapter(1, 1, m)))

        def prepare():
            return member_matrix(mats_t[1], col(), adapter(0, 1, m))

        def finish(product):
            grad = product.astype(BF16) * slope(rises[lax.rem(m + SLOTS - 1, SLOTS)], act1[m])
            wide_rows[2, 0, pl.ds(m, 1), :] = 0.5 * jnp.sum(
                grad.astype(F32), axis=0, keepdims=True
            )
            act1[m] = grad
            return grad

        return finish(contract(keep1[m], prepare(), 1, 0))

    begin_second_small()

    def back_first(i, carry):
        m = 2 * i
        for k in range(2):
            rise_copy(m + k, False).wait()
        at(i, back_steps)
        for k in range(2):
            back_units(m + k)

        @pl.when(i < members // 2 - 2)
        def _():
            for k in range(SLOTS, SLOTS + 2):
                rise_copy(m + k, False).start()

        return carry

    nearly = inner > 1
    back_steps = [(2, begin_second_wide)]
    if nearly:
        back_steps += [(4, second_s.add_near), (6, second_w.add_near)]
    lax.fori_loop(0, members // 2, back_first, 0)

    def product_pass(number, steps):
        cols = halves[number]

        def unit(m):
            def finish(product):
                for k in range(2):
                    row_sum, out_grad = spread_product(
                        product[:, k * half_cols : (k + 1) * half_cols],
                        mats[0, :, cols],
                        column(adapter(0, 0, m + k)),
                        0.5 * adapter(1, 0, m + k, cols),
                        grad_w.at[:, cols],
                    )
                    wide_rows[1, 0, pl.ds(m + k, 1), cols] = out_grad
                    in_grad = row_of(row_sum)
                    if number:
                        in_grad = in_grad + wide_rows[0, 0, pl.ds(m + k, 1), :]
                    wide_rows[0, 0, pl.ds(m + k, 1), :] = in_grad

            def product(_):
                grads = [act1[m + k, :, cols] for k in range(2)]
                low = jnp.concatenate(grads, axis=1)
                fill = jnp.zeros((embed_t.shape[1] - rows, low.shape[1]), BF16)
                return contract(embed_t[...], jnp.concatenate([low, fill], axis=0), 1, 0)

            return nothing, product, finish

        def body(i, carry):
            at(i, steps)
            run_units([unit(8 * i + k) for k in range(0, 8, 2)])
            return carry

        lax.fori_loop(0, members // 8, body, 0)

    if nearly:
        product_pass(0, [(0, second_s.add_far), (1, second_w.add_far)])
    else:
        product_pass(0, [(0, second_s.add_far), (1, second_w.add_far)])
    take_low = send_half(1, halves[0])

    def begin_low():
        put(block0_x.buf, 0, take_low())
        block0_x.start()
        if nearly:
            second_w.spread()

    product_pass(1, ([(0, second_s.spread)] if nearly else []) + [(1, begin_low)])
    take_high = send_half(2, halves[1])
    for i in range(3):
        put(first_x.buf, i * across, wide_rows[i, 0])
    clear(first_x.buf, 3 * across)
    first_x.start()

    def into_embedding(m, cols):
        return member_matrix(
            mats_t[0, :, cols], column(0.5 * adapter(1, 0, m)), adapter(0, 0, m, cols)
        )

    def embedding_pass(side, cols, steps):
        def body(i, carry):
            at(i, steps)
            members_here = [4 * i + k for k in range(4)]
            low = [into_embedding(m, cols) for m in members_here]
            grads = [act1[m] for m in members_here]
            grad_e[side] += contract(
                jnp.concatenate(grads, axis=1), jnp.concatenate(low, axis=0), 1, 0
            )
            return carry

        lax.fori_loop(0, members // 4, body, 0)

    def begin_high():
        put(block1_x.buf, 0, take_high())
        block1_x.start()

    embedding_pass(0, their_cols, [(1, begin_high), (2, block0_x.add_far), (3, first_x.add_far)])
    stage_e[...] = grad_e[0].astype(BF16)
    copy_ge = to_partner(stage_e, pair_e, 14)
    copy_ge.start()
    embedding_pass(1, my_cols, [(1, block1_x.add_far)])
    copy_ge.wait()
    grad_own = (grad_e[1] + pair_e[...].astype(F32)).T.astype(BF16)
    table_grad = contract(grad_own, one_hot(), 1, 1)
    for f in range(own_feat):
        block = table_grad[edim * f : edim * (f + 1), bins * f : bins * (f + 1)]
        table_x.buf[f] = jnp.concatenate(
            [block, jnp.zeros((edim, LANES - bins), F32)], axis=1
        ).astype(BF16)
    clear(table_x.buf, own_feat)
    table_x.start()
    table_x.add_far()
    second_s.finish()
    second_w.finish()
    if inner:
        part = misc_out.at[pl.ds(0, n_rows - 1)]
        for side in range(2):
            pltpu.make_async_copy(part, part, sems.at[second_s.first + 8 + side]).wait()
    table_x.finish()
    block0_x.finish()
    first_x.finish()
    block1_x.finish()


def adamw(value, grad, first, second, rate):
    first_new = DECAY_FIRST * first + (1.0 - DECAY_FIRST) * grad
    second_new = DECAY_SECOND * second + (1.0 - DECAY_SECOND) * grad * grad
    first_hat = first_new / (1.0 - DECAY_FIRST**STEP)
    second_hat = second_new / (1.0 - DECAY_SECOND**STEP)
    value_new = value - rate * (first_hat / (jnp.sqrt(second_hat) + EPSILON) + WEIGHT_DECAY * value)
    return value_new, first_new, second_new


def update_kernel(*refs):
    count = 23
    ins, outs = refs[:count], refs[count : count + 18]
    held = refs[count + 18 : count + 18 + count]
    made = refs[count + 18 + count : count + 18 + count + 18]
    grad_ref, in_sems, out_sems = refs[-3:]
    copies = [
        pltpu.make_async_copy(src, dst, in_sems.at[i])
        for i, (src, dst) in enumerate(zip(ins, held))
    ]
    for copy in copies:
        copy.start()

    def get(i):
        copies[i].wait()
        return held[i]

    stores = []

    def send(i):
        store = pltpu.make_async_copy(made[i], outs[i], out_sems.at[i])
        store.start()
        stores.append(store)

    mem = lax.axis_index("mem")
    wide = get(0)
    width = grad_ref.shape[0]
    across = width // LANES
    half = width // 2
    tiles = half // TILE * across
    for c in range(2):
        for i in range(half // TILE):
            for j in range(across):
                split = j // 2 * tiles + c * tiles // 2 + i * 2 + j % 2
                whole = c * tiles + i * across + j
                grad_ref[
                    c * half + i * TILE : c * half + (i + 1) * TILE, j * LANES : (j + 1) * LANES
                ] = wide[jnp.where(mem == 0, split, whole)]
    low = grad_ref[...]
    moment = get(1)
    moment_new = MOMENTUM * moment[...] + low.astype(F32)
    made[6][...] = moment_new
    send(6)
    root_l = get(2)
    left = contract(root_l[...].astype(BF16), moment_new.astype(BF16), 1, 0)
    root_r = get(3)
    direction = contract(left.astype(BF16), root_r[...].astype(BF16), 1, 0)
    matrix = get(4)
    made[5][...] = matrix[...] - LR_SHAMPOO * direction
    send(5)
    stat_l = get(5)
    made[7][...] = DECAY_STAT * stat_l[...] + contract(low, low, 1, 1)
    send(7)
    stat_r = get(6)
    made[8][...] = DECAY_STAT * stat_r[...] + contract(low, low, 0, 0)
    send(8)

    def apply(group, news, index, grad, rate):
        results = adamw(group[0][index], grad, group[1][index], group[2][index], rate)
        for new, result in zip(news, results):
            new[index] = result

    second, first, table_grad, misc = [get(i) for i in range(7, 11)]
    adapt = [get(i) for i in range(11, 14)]
    members = adapt[0].shape[2]
    head_tiles = members // 2 * across
    for l, (tiles_ref, place) in enumerate(((first, 0), (second, head_tiles))):
        for i in range(3):
            for j in range(across):
                where = (i, l, slice(None), pl.ds(j * LANES, LANES))
                grad = tiles_ref[place + i * across + j].astype(F32)
                apply(adapt, made[9:12], where, grad, LR_ADAPTER)
    for i in range(9, 12):
        send(i)
    head = [get(i) for i in range(14, 17)]
    classes = head[0].shape[1]
    for m in range(0, members, 2):
        for j in range(across):
            pair = second[m // 2 * across + j].astype(F32)
            for k in range(2):
                where = (m + k, slice(None), pl.ds(j * LANES, LANES))
                part = pair[k * classes : (k + 1) * classes]
                apply(head, made[12:15], where, part, LR_HEAD)
    for i in range(12, 15):
        send(i)
    table = [get(i) for i in range(17, 20)]
    own_feat, bins = table[0].shape[0], table[0].shape[2]
    for f in range(own_feat):
        apply(table, made[2:5], f, table_grad[f][:, :bins].astype(F32), LR_TABLE)
    for i in range(2, 5):
        send(i)
    bias = [get(i) for i in range(20, 23)]
    total = misc[0]
    for k in range(1, misc.shape[0]):
        total = total + misc[k]
    apply(bias, made[15:18], Ellipsis, total[:, :members], LR_BIAS)
    made[0][...] = jnp.broadcast_to(total[0:1, members : members + 1], made[0].shape)
    made[1][...] = jnp.broadcast_to(total[0:1, members + 1 : members + 2], made[1].shape)
    for i in (0, 1, 15, 16, 17):
        send(i)
    for store in stores:
        store.wait()


def shards(
    n_rows,
    bin_index,
    labels,
    row_weight,
    bin_table,
    table_first,
    table_second,
    weights,
    weights_moment,
    stat_left,
    stat_right,
    root_left,
    root_right,
    adapters,
    adapter_first,
    adapter_second,
    head_weight,
    head_first,
    head_second,
    head_bias,
    bias_first,
    bias_second,
):
    rows = bin_index.shape[0]
    width = weights.shape[2]
    members, _, classes = head_weight.shape
    own_feat = bin_table.shape[0]
    across = width // LANES
    half_tiles = width // 2 // TILE * across
    head_tiles = members // 2 * across
    inner = 0 if SHARES % n_rows else INNER
    fit = lambda count: -(-count // SHARES) * SHARES
    sizes = (
        (inner, half_tiles),
        (inner, fit(head_tiles + 3 * across)),
        (1, fit(own_feat)),
        (1, half_tiles // 2),
        (1, half_tiles // 2),
        (1, fit(3 * across)),
    )

    def tiles(*shape, kind=BF16):
        return pltpu.VMEM((*shape, TILE, LANES), kind)

    stages = []
    for i, (near, count) in enumerate(sizes):
        if inner:
            far = n_rows // near
            block = count // near
            kind = F32 if near > 1 else BF16
            stages += [
                tiles(count),
                tiles(max(near - 1, 1), block if near > 1 else 1),
                tiles(block if near > 1 else 1, kind=kind),
                tiles(far - 1, block // far, kind=kind),
                tiles(count, kind=F32 if i == 1 else BF16),
            ]
        else:
            stages += [tiles(count)] + [tiles(1)] * 4
    tables = [jnp.swapaxes(x, 1, 2) for x in (bin_table, table_first, table_second)]
    heads = [jnp.swapaxes(x, 1, 2) for x in (head_weight, head_first, head_second)]
    biases = [jnp.transpose(x) for x in (head_bias, bias_first, bias_second)]
    squares = [x[0] for x in (weights, weights_moment, stat_left, stat_right, root_left, root_right)]
    in_vmem = pl.BlockSpec(memory_space=pltpu.VMEM)
    in_hbm = pl.BlockSpec(memory_space=pl.ANY)
    struct = jax.ShapeDtypeStruct
    grad_tiles = lambda count: struct((count, TILE, LANES), BF16)
    big = pltpu.VMEM((members, rows, width), BF16)
    wide, second, first, table, misc, _, _ = pl.pallas_call(
        functools.partial(step_kernel, n_rows, inner),
        out_shape=(
            grad_tiles(2 * half_tiles),
            struct((sizes[1][1], TILE, LANES), F32),
            grad_tiles(sizes[5][1]),
            grad_tiles(sizes[2][1]),
            struct((n_rows if inner else 1, classes, LANES), F32),
            struct((members, rows, width), BF16),
            struct((members, rows, width), BF16),
        ),
        in_specs=[in_vmem] * 8,
        out_specs=(in_vmem,) * 5 + (in_hbm,) * 2,
        scratch_shapes=[
            pltpu.VMEM((rows, width), BF16),
            pltpu.VMEM((2, width, width), F32),
            pltpu.VMEM((2, width, width), BF16),
            big,
            big,
            pltpu.VMEM((members, classes, rows), F32),
            pltpu.VMEM((SLOTS, rows, width), BF16),
            pltpu.VMEM((SLOTS, rows, width), BF16),
            pltpu.VMEM((width, -(-rows // LANES) * LANES), BF16),
            pltpu.VMEM((3 * width // 2, width), BF16),
            pltpu.VMEM((rows, width // 2), BF16),
            pltpu.VMEM((2, rows, width // 2), F32),
            pltpu.VMEM((width, width), F32),
            pltpu.VMEM((2, classes, rows), F32),
            pltpu.VMEM((2, 8, rows), F32),
            pltpu.VMEM((rows, width // 2), BF16),
            pltpu.VMEM((3 * width // 2, width), BF16),
            pltpu.VMEM((3, 2, members, width), F32),
            pltpu.VMEM((members, classes, width), F32),
            pltpu.VMEM((classes, LANES), F32),
            pltpu.SemaphoreType.DMA((16 + 6 * EXCHANGE_SEMS,)),
            pltpu.SemaphoreType.DMA((2 * SLOTS,)),
            *stages,
        ],
        compiler_params=pltpu.CompilerParams(
            collective_id=0, has_side_effects=True, vmem_limit_bytes=64 * 2**20
        ),
        name="step",
    )(
        jnp.transpose(bin_index),
        labels[None],
        row_weight[None],
        tables[0],
        squares[0],
        adapters,
        heads[0],
        biases[0],
    )
    if not inner:
        wide, second, first, table, misc = lax.psum(
            (wide.astype(F32), second.astype(F32), first.astype(F32), table.astype(F32), misc),
            "rows",
        )
        first, table = [x.astype(BF16) for x in (first, table)]
        halves = lax.all_gather(wide.astype(BF16), "mem").reshape(2, 2, half_tiles, TILE, LANES)
        parts = halves[:, 0].reshape(2, 2, half_tiles // 2, TILE, LANES)
        wide = jnp.where(
            lax.axis_index("mem") == 0,
            jnp.swapaxes(parts, 0, 1).reshape(-1, TILE, LANES),
            halves[:, 1].reshape(-1, TILE, LANES),
        )
    one = struct((1, LANES), F32)
    like = lambda x: struct(x.shape, F32)
    ins = (
        wide,
        squares[1],
        squares[4],
        squares[5],
        squares[0],
        squares[2],
        squares[3],
        second,
        first,
        table,
        misc,
        adapters,
        adapter_first,
        adapter_second,
        *heads,
        *tables,
        *biases,
    )
    results = (
        one,
        one,
        *[like(x) for x in tables],
        *[like(squares[0])] * 4,
        *[like(adapters)] * 3,
        *[like(x) for x in heads],
        *[like(x) for x in biases],
    )
    outs = pl.pallas_call(
        update_kernel,
        out_shape=results,
        in_specs=[in_hbm] * len(ins),
        out_specs=(in_hbm,) * len(results),
        scratch_shapes=[pltpu.VMEM(x.shape, x.dtype) for x in ins]
        + [pltpu.VMEM(x.shape, x.dtype) for x in results]
        + [
            pltpu.VMEM((width, width), BF16),
            pltpu.SemaphoreType.DMA((len(ins),)),
            pltpu.SemaphoreType.DMA((len(results),)),
        ],
        compiler_params=pltpu.CompilerParams(vmem_limit_bytes=60 * 2**20),
        name="update",
    )(*ins)
    back = lambda xs: [jnp.swapaxes(x, 1, 2) for x in xs]
    return (
        outs[0][0, 0],
        outs[1][0, 0],
        *back(outs[2:5]),
        *[x[None] for x in outs[5:9]],
        *outs[9:12],
        *back(outs[12:15]),
        *[jnp.transpose(x) for x in outs[15:18]],
    )


def solution(mesh):
    tables = P("mem", None, None)
    adapt = P(None, None, "mem", None)
    pair = P("mem", None)
    return jax.shard_map(
        functools.partial(shards, mesh.shape["rows"]),
        mesh=mesh,
        in_specs=(P("rows", "mem"), P("rows"), P("rows"))
        + (tables,) * 9
        + (adapt,) * 3
        + (tables,) * 3
        + (pair,) * 3,
        out_specs=(P(), P()) + (tables,) * 7 + (adapt,) * 3 + (tables,) * 3 + (pair,) * 3,
        check_vma=False,
    )
```

```python
import functools

import jax
import jax.numpy as jnp
from jax import lax
from jax.experimental import pallas as pl
from jax.experimental.pallas import tpu as pltpu
from jax.sharding import PartitionSpec as P

STEP = 10
LR_TABLE = 1.0
LR_ADAPTER = 0.7
LR_HEAD = 0.15
LR_BIAS = 0.5
LR_SHAMPOO = 4.0
DECAY_FIRST = 0.9
DECAY_SECOND = 0.999
DECAY_STAT = 0.95
MOMENTUM = 0.9
WEIGHT_DECAY = 0.01
EPSILON = 1e-08

F32 = jnp.float32
BF16 = jnp.bfloat16
MESH = pl.DeviceIdType.MESH
LANES = 128
TILE = 16
SHARES = 16
INNER = 4


def contract(a, b, a_dim, b_dim):
    return lax.dot_general(
        a, b, (((a_dim,), (b_dim,)), ((), ())), preferred_element_type=F32
    )


def column(row):
    return jnp.broadcast_to(row, (LANES, row.shape[1])).T


def member_matrix(matrix, in_column, out_row):
    parts = []
    for start in range(0, matrix.shape[1], LANES):
        cols = slice(start, start + LANES)
        parts.append((matrix[:, cols].astype(F32) * in_column * out_row[:, cols]).astype(BF16))
    return jnp.concatenate(parts, axis=1)


def slope(rise, active):
    return rise + active * (2.0 - rise)


def spread_product(product, matrix, in_column, half_row, total):
    row_sum = None
    out_grads = []
    for start in range(0, matrix.shape[1], LANES):
        cols = slice(start, start + LANES)
        part = product[: matrix.shape[0], cols]
        scale = half_row[:, cols]
        mixed = matrix[:, cols] * part
        total[:, cols] += in_column * part * scale
        out_grads.append(jnp.sum(in_column * mixed, axis=0, keepdims=True))
        mixed = mixed * scale
        row_sum = mixed if row_sum is None else row_sum + mixed
    return row_sum, 0.5 * jnp.concatenate(out_grads, axis=1)


def row_of(sums):
    return jnp.sum(sums.T, axis=0, keepdims=True)


def run_units(units):
    ready = units[0][0]()
    result = units[0][1](ready)
    ready = units[1][0]() if len(units) > 1 else None
    for k, (_, _, finish) in enumerate(units):
        following = None
        if k + 1 < len(units):
            following = units[k + 1][1](ready)
            if k + 2 < len(units):
                ready = units[k + 2][0]()
        finish(result)
        result = following


def once(function):
    held = []

    def get():
        if not held:
            held.append(function())
        return held[0]

    return get


def nothing(*_):
    return None


class Exchange:
    def __init__(self, sems, first_sem, n_rows, inner, buf, near, mid, far, done, out, base, core):
        self.sems, self.first = sems, first_sem
        self.inner, self.outer = inner, n_rows // inner
        self.buf, self.near, self.mid, self.far, self.done = buf, near, mid, far, done
        self.out, self.base, self.core = out, base, core
        self.tiles = buf.shape[0]
        self.per = self.tiles // n_rows
        self.block = self.per * self.outer
        self.mem = lax.axis_index("mem")
        self.me = lax.axis_index("rows")
        self.my_in = lax.rem(self.me, inner)
        self.my_out = self.me // inner
        self.here = (self.my_in * self.outer + self.my_out) * self.per

    def send(self, src, dst, sem, core, peer):
        pltpu.make_async_remote_copy(
            src_ref=src,
            dst_ref=dst,
            send_sem=self.sems.at[self.first + 2 * sem],
            recv_sem=self.sems.at[self.first + 2 * sem + 1],
            device_id=(core, peer),
            device_id_type=MESH,
        ).start()

    def wait(self, tiles, sem, received):
        src = self.buf if self.inner == 1 else self.mid
        part = (self.buf, src, self.done, self.out)[sem].at[pl.ds(0, tiles)]
        pltpu.make_async_copy(part, part, self.sems.at[self.first + 2 * sem + received]).wait()

    def each_near(self, step):
        def body(k, carry):
            peer = lax.rem(self.my_in + k, self.inner)
            step(k, peer, self.my_out * self.inner + peer)
            return carry

        lax.fori_loop(1, self.inner, body, 0, unroll=True)

    def each_far(self, step):
        def body(k, carry):
            peer = lax.rem(self.my_out + k, self.outer)
            step(k, peer, peer * self.inner + self.my_in)
            return carry

        lax.fori_loop(1, self.outer, body, 0, unroll=True)

    def start(self):
        if self.inner == 1:
            self.send_far(self.buf)
        else:
            self.each_near(
                lambda k, peer, device: self.send(
                    self.buf.at[pl.ds(peer * self.block, self.block)],
                    self.near.at[k - 1],
                    0,
                    self.mem,
                    device,
                )
            )

    def add_near(self):
        self.wait((self.inner - 1) * self.block, 0, 1)
        total = self.buf[pl.ds(self.my_in * self.block, self.block)].astype(F32)
        for k in range(self.inner - 1):
            total = total + self.near[k].astype(F32)
        self.mid[...] = total.astype(self.mid.dtype)
        self.send_far(self.mid)

    def send_far(self, src):
        self.each_far(
            lambda k, peer, device: self.send(
                src.at[pl.ds(peer * self.per, self.per)], self.far.at[k - 1], 1, self.mem, device
            )
        )

    def add_far(self):
        src = self.buf if self.inner == 1 else self.mid
        self.wait((self.outer - 1) * self.per, 1, 1)

        def body(k, total):
            return total + self.far[k].astype(F32)

        own = src[pl.ds(self.my_out * self.per, self.per)].astype(F32)
        total = lax.fori_loop(0, self.outer - 1, body, own, unroll=True)
        part = pl.ds(self.here, self.per)
        self.done[part] = total.astype(self.done.dtype)
        if self.inner == 1:
            self.hand_out(self.here, self.per, self.each_far)
        else:
            self.each_far(
                lambda k, peer, device: self.send(
                    self.done.at[part], self.done.at[part], 2, self.mem, device
                )
            )

    def spread(self):
        self.wait((self.outer - 1) * self.per, 2, 1)
        self.hand_out(self.my_in * self.block, self.block, self.each_near)

    def hand_out(self, at, size, each):
        src = self.done.at[pl.ds(at, size)]
        if self.core is None:
            dst = self.out.at[pl.ds(self.base + at, size)]
            each(lambda k, peer, device: self.send(src, dst, 3, self.mem, device))
            dst[...] = src[...]
        else:
            dst = self.out.at[pl.ds(self.base + self.mem * self.tiles + at, size)]
            each(lambda k, peer, device: self.send(src, dst, 3, self.core, device))

            @pl.when(self.mem == self.core)
            def _():
                dst[...] = src[...]

            @pl.when(self.mem != self.core)
            def _():
                self.send(src, dst, 3, self.core, self.me)

    def finish(self):
        if self.inner > 1:
            self.wait((self.inner - 1) * self.block, 0, 0)
            self.wait((self.outer - 1) * self.per, 2, 0)
            own, peers = self.block, self.inner - 1
        else:
            own, peers = self.per, self.outer - 1
        self.wait((self.outer - 1) * self.per, 1, 0)
        if self.core is None:
            self.wait(self.tiles - own, 3, 1)
            self.wait(peers * own, 3, 0)
        else:

            @pl.when(self.mem == self.core)
            def _():
                self.wait(2 * self.tiles - own, 3, 1)
                self.wait(peers * own, 3, 0)

            @pl.when(self.mem != self.core)
            def _():
                self.wait((peers + 1) * own, 3, 0)


EXCHANGE_SEMS = 10


class Handover(Exchange):
    def __init__(self, buf, out, base):
        self.buf, self.out, self.base = buf, out, base

    def start(self):
        self.out[pl.ds(self.base, self.buf.shape[0])] = self.buf[...].astype(self.out.dtype)

    def add_near(self):
        pass

    add_far = spread = finish = add_near


SLOTS = 4


def step_kernel(
    n_rows,
    inner,
    bins_ref,
    label_ref,
    weight_ref,
    table_ref,
    matrix_ref,
    adapt_ref,
    head_ref,
    bias_ref,
    wide_out,
    second_out,
    first_out,
    table_out,
    misc_out,
    act2,
    rise1,
    embed,
    mats,
    mats_t,
    keep1,
    act1,
    prob,
    slots,
    embed_t,
    stage_w,
    grad_e,
    grad_w,
    sums,
    spreads,
    result_a,
    result_b,
    pair_e,
    pair_w,
    wide_rows,
    head_grads,
    misc,
    sems,
    slot_sems,
    *stages,
):
    mem = lax.axis_index("mem")
    me = lax.axis_index("rows")
    other = 1 - mem
    rows, width = embed.shape
    members, classes = head_ref.shape[0], head_ref.shape[1]
    own_feat, edim, bins = table_ref.shape
    own_cols = own_feat * edim
    total_rows = rows * n_rows
    total_members = 2 * members
    half_rows = half_cols = width // 2
    across = width // LANES
    halves = [slice(0, half_cols), slice(half_cols, width)]
    my_cols = pl.ds(pl.multiple_of(mem * own_cols, own_cols), own_cols)
    their_cols = pl.ds(pl.multiple_of(other * own_cols, own_cols), own_cols)
    their_half = pl.ds(pl.multiple_of(other * half_rows, half_rows), half_rows)
    my_half = pl.ds(pl.multiple_of(mem * half_rows, half_rows), half_rows)

    barrier = pltpu.get_barrier_semaphore()
    line = me * 2 + mem

    def greet(k, carry):
        peer = lax.rem(line + k, 2 * n_rows)
        pl.semaphore_signal(
            barrier, inc=1, device_id=(lax.rem(peer, 2), peer // 2), device_id_type=MESH
        )
        return carry

    load = pltpu.make_async_copy(matrix_ref, result_a.at[pl.ds(0, width)], slot_sems.at[0])
    load.start()
    lax.fori_loop(1, 2 * n_rows, greet, 0)

    def to_partner(src, dst, sem):
        return pltpu.make_async_remote_copy(
            src_ref=src,
            dst_ref=dst,
            send_sem=sems.at[sem],
            recv_sem=sems.at[sem + 1],
            device_id=(other, me),
            device_id_type=MESH,
        )

    def adapter(kind, layer, m, cols=slice(None)):
        return adapt_ref[kind, layer, pl.ds(m, 1), cols]

    def one_hot():
        parts = []
        for f in range(own_feat):
            ids = lax.broadcasted_iota(jnp.int32, (bins, rows), 0)
            parts.append((bins_ref[f : f + 1, :] == ids).astype(F32))
        return jnp.concatenate(parts, axis=0).astype(BF16)

    blocks = []
    for f in range(own_feat):
        pads = [table_ref[f]]
        if f > 0:
            pads.insert(0, jnp.zeros((edim, bins * f), F32))
        if f < own_feat - 1:
            pads.append(jnp.zeros((edim, bins * (own_feat - 1 - f)), F32))
        blocks.append(jnp.concatenate(pads, axis=1))
    lookup = jnp.concatenate(blocks, axis=0).astype(BF16)
    embed[:, my_cols] = contract(lookup, one_hot(), 1, 0).T.astype(BF16)
    load.wait()
    own_low = result_a[0:width, :].astype(BF16)
    outgoing = stage_w.at[pl.ds(0, width), :]
    outgoing[...] = own_low
    mats[mem] = own_low.astype(F32)

    grad_w[...] = jnp.zeros_like(grad_w)
    grad_e[...] = jnp.zeros_like(grad_e)
    pl.semaphore_wait(barrier, 2 * n_rows - 1)
    copy_e = to_partner(embed.at[:, my_cols], embed.at[:, my_cols], 0)
    copy_w = to_partner(outgoing, pair_w.at[pl.ds(0, width), :], 2)
    copy_e.start()
    copy_w.start()
    copy_w.wait()
    mats[other] = pair_w[0:width, :].astype(F32)
    copy_e.wait()

    def scaled(layer, m, col, cols):
        return member_matrix(mats[layer, :, cols], col(), 0.5 * adapter(1, layer, m, cols))

    def first_units(m, slot):
        col = once(lambda: column(adapter(0, 0, m)))

        def unit(cols):
            def finish(product):
                half = product + 0.5 * adapter(2, 0, m, cols)
                rise = 1.0 + jnp.tanh(half)
                act1[m, :, cols] = (half * rise).astype(BF16)
                slots[SLOTS + slot, :, cols] = rise.astype(BF16)

            return (
                lambda: scaled(0, m, col, cols),
                lambda low: contract(embed[...], low, 1, 0),
                finish,
            )

        return [unit(cols) for cols in halves]

    def second_units(m, slot):
        col = once(lambda: column(adapter(0, 1, m)))

        def unit(cols):
            def finish(product):
                half = product + 0.5 * adapter(2, 1, m, cols)
                rise = 1.0 + jnp.tanh(half)
                slots[slot, :, cols] = (half * rise).astype(BF16)
                keep1[m, :, cols] = rise.astype(BF16)

            return (
                lambda: scaled(1, m, col, cols),
                lambda low: contract(act1[m], low, 1, 0),
                finish,
            )

        return [unit(cols) for cols in halves]

    def head_unit(m, slot):

        def finish(logits):
            lane = lax.broadcasted_iota(jnp.int32, (classes, members), 1)
            shift = jnp.sum(jnp.where(lane == m, bias_ref[...], 0.0), axis=1, keepdims=True)
            logits = logits + shift
            power = jnp.exp(logits - jnp.max(logits, axis=0, keepdims=True))
            share = power / jnp.sum(power, axis=0, keepdims=True)
            prob[m] = share
            sums[0] += share

        return (nothing, lambda _: contract(head_ref[m].astype(BF16), slots[slot], 1, 1), finish)

    def keep(array, m, slot):
        return pltpu.make_async_copy(slots.at[slot], array.at[m], slot_sems.at[slot])

    def fetch(array, m, slot):
        return pltpu.make_async_copy(array.at[m], slots.at[slot], slot_sems.at[slot])

    def keep_active(m):
        return keep(act2, m, lax.rem(m, SLOTS))

    def keep_rise(m):
        return keep(rise1, m, SLOTS + lax.rem(m + SLOTS - 2, SLOTS))

    def turn_of(turn):
        return lax.rem(turn + members - SLOTS, members)

    def fetch_active(turn):
        return fetch(act2, turn_of(turn), lax.rem(turn, 2 * SLOTS))

    def fetch_rise(m):
        return fetch(rise1, m, lax.rem(m, 2 * SLOTS))

    sums[0] = jnp.zeros((classes, rows), F32)
    run_units(first_units(0, SLOTS - 2) + first_units(1, SLOTS - 1))
    for m in range(2):
        keep_rise(m).start()

    def forward(m, slot, with_next):
        if with_next:
            units = []
            for k in range(2):
                left, right = second_units(m + k, slot + k)
                one, two = first_units(m + k + 2, slot + k)
                units += [left, one, right, two, head_unit(m + k, slot + k)]
        else:
            left, right = second_units(m, slot)
            one, two = second_units(m + 1, slot + 1)
            units = [left, right, one, head_unit(m, slot), two]
            units += [(nothing,) * 3, head_unit(m + 1, slot + 1)]
        run_units(units)
        if with_next:
            for k in range(2):
                keep_rise(m + k + 2).start()

            @pl.when(m < members - SLOTS)
            def _():
                for k in range(2):
                    keep_active(m + k).start()

    def forward_step(i, carry):
        m = 2 * i

        @pl.when(i >= 1)
        def _():
            keep_rise(m - 2).wait()
            keep_rise(m - 1).wait()

        @pl.when(i >= 2)
        def _():
            keep_active(m - 4).wait()
            keep_active(m - 3).wait()

        forward(m, 2 * lax.rem(i, 2), True)
        return carry

    lax.fori_loop(0, members // 2 - 1, forward_step, 0)
    keep_active(members - 6).wait()
    keep_active(members - 5).wait()
    forward(members - 2, (members - 2) % SLOTS, False)
    copy_p = to_partner(sums.at[0], sums.at[1], 4)
    copy_p.start()
    for m in range(members - 4, members):
        keep_rise(m).wait()
    fetch_active(SLOTS).start()
    embed_t[...] = jnp.zeros_like(embed_t)
    embed_t[0:width, 0:rows] = embed[...].T
    embed_t[width : width + TILE, 0:rows] = jnp.ones((TILE, rows), BF16)
    for layer in range(2):
        mats_t[layer] = mats[layer].astype(BF16).T
    copy_p.wait()
    mean = (sums[0] + sums[1]) * (1.0 / total_members)
    target = (
        label_ref[...] == lax.broadcasted_iota(jnp.int32, (classes, rows), 0)
    ).astype(F32)
    picked = jnp.sum(mean * target, axis=0, keepdims=True)
    row_weight = weight_ref[...]
    factor = row_weight / (total_rows * total_members * picked)
    loss = jnp.sum(row_weight * -jnp.log(picked), axis=1, keepdims=True)

    spreads[0] = jnp.zeros_like(spreads[0])
    misc[...] = jnp.zeros_like(misc)
    spot = lax.broadcasted_iota(jnp.int32, (classes, LANES), 1)

    def logit_units(m, slot):

        @once
        def grads():
            share = prob[m]
            own_pick = jnp.sum(share * target, axis=0, keepdims=True)
            gap = share - mean
            spreads[0, 0:1] += jnp.sum(gap * gap, axis=0, keepdims=True)
            grad = -(factor * own_pick) * (target - share)
            return grad.astype(BF16), grad.T.astype(BF16), jnp.sum(grad, axis=1, keepdims=True)

        def unit(cols):
            def finish(product):
                keep1[m, :, cols] = product.astype(BF16) * slope(
                    keep1[m, :, cols], slots[slot, :, cols]
                )

            return (
                nothing,
                lambda _: contract(grads()[1], head_ref[m, :, cols].astype(BF16), 1, 0),
                finish,
            )

        def finish(product):
            head_grads[m] = product
            misc[...] = jnp.where(spot == m, grads()[2], misc[...])

        return [unit(cols) for cols in halves] + [
            (nothing, lambda _: contract(grads()[0], slots[slot], 1, 0), finish)
        ]

    def product_unit(m, number, turned, held):
        cols = halves[number]

        def product(_):
            result = contract(turned(), keep1[m, :, cols], 1, 0)
            if held is not None:
                held[:, 0:half_cols] = result
            return result

        return turned, product, nothing if held is not None else lambda p: split_up(m, number, p)

    def split_up(m, number, product):
        cols = halves[number]
        wide_rows[2, 1, pl.ds(m, 1), cols] = 0.5 * product[width : width + 1, :]
        row_sum, out_grad = spread_product(
            product,
            mats[1, :, cols],
            column(adapter(0, 1, m)),
            0.5 * adapter(1, 1, m, cols),
            grad_w.at[:, cols],
        )
        wide_rows[1, 1, pl.ds(m, 1), cols] = out_grad
        in_grad = row_of(row_sum)
        if number:
            in_grad = in_grad + wide_rows[0, 1, pl.ds(m, 1), :]
        wide_rows[0, 1, pl.ds(m, 1), :] = in_grad

    def held_split(m):
        return nothing, nothing, lambda _: split_up(m, 1, result_a[:, 0:half_cols])

    ones = jnp.ones((TILE, rows), BF16)

    def back_second(turn, with_next):
        units = []
        slot = lax.rem(turn, 2 * SLOTS)
        for k in range(SLOTS):
            m = turn_of(turn + k)
            turned = once(lambda m=m: jnp.concatenate([act1[m].T, ones], axis=0))
            left = product_unit(m, 0, turned, None)
            right = product_unit(m, 1, turned, result_a)
            held = held_split(turn_of(jnp.maximum(turn + k - 1, 0)))
            if k < SLOTS - 1 or with_next:
                after = turn_of(turn + k + 1)
                one, two, head = logit_units(after, lax.rem(turn + k + 1, 2 * SLOTS))
                units += [held, left, one, right, two, head]
            else:
                units += [held, left, right]
        run_units(units)

    def back_second_step(i, carry):
        turn = SLOTS * i

        @pl.when(i >= 1)
        def _():
            for k in range(SLOTS - 1):
                fetch_active(turn + 1 + k).wait()

        fetch_active(turn + SLOTS).wait()
        for k in range(SLOTS - 1):
            fetch_active(turn + SLOTS + 1 + k).start()

        @pl.when(i < members // SLOTS - 2)
        def _():
            fetch_active(turn + 2 * SLOTS).start()

        back_second(turn, True)
        return carry

    run_units(logit_units(members - SLOTS, 0))
    result_a[...] = jnp.zeros_like(result_a)
    wide_rows[0, 1] = jnp.zeros((members, width), F32)
    lax.fori_loop(0, members // SLOTS - 1, back_second_step, 0)
    for m in range(members - SLOTS + 1, members):
        fetch_active(m).wait()
    for m in range(SLOTS):
        fetch_rise(m).start()
    back_second(members - SLOTS, False)
    split_up(members - SLOTS - 1, 1, result_a[:, 0:half_cols])

    def put(buf, first_tile, block):
        down, broad = block.shape[0] // TILE, block.shape[1] // LANES
        for i in range(down):
            for j in range(broad):
                buf[first_tile + i * broad + j] = block[
                    i * TILE : (i + 1) * TILE, j * LANES : (j + 1) * LANES
                ].astype(BF16)

    def clear(buf, first_tile):
        for t in range(first_tile, buf.shape[0]):
            buf[t] = jnp.zeros((TILE, LANES), BF16)

    half_tiles = half_rows // TILE * across
    plan = (
        (inner, wide_out, 0, half_tiles, 1),
        (inner, second_out, 0, 0, None),
        (1, table_out, 0, 0, None),
        (1, wide_out, 0, 0, 0),
        (1, wide_out, half_tiles, half_tiles // 2, 0),
        (1, first_out, 0, 0, None),
    )
    exchanges = []
    for i, (near, out, base, own_base, core) in enumerate(plan):
        refs = stages[5 * i : 5 * i + 5]
        if inner:
            first_sem = 16 + EXCHANGE_SEMS * i
            exchanges.append(Exchange(sems, first_sem, n_rows, near, *refs, out, base, core))
        else:
            exchanges.append(Handover(refs[0], out, own_base))
    second_w, second_s, table_x, block0_x, block1_x, first_x = exchanges

    def half_exchange(slot, cols, exchange):
        broad = cols.stop - cols.start
        src = stage_w.at[pl.ds(half_rows * slot, half_rows), pl.ds(0, broad)]
        dst = pair_w.at[pl.ds(half_rows * slot, half_rows), pl.ds(0, broad)]

        def copy():
            return to_partner(src, dst, 8 + 2 * slot)

        def send():
            src[...] = grad_w[their_half, cols].astype(BF16)
            copy().start()

        def begin():
            copy().wait()
            put(exchange.buf, 0, grad_w[my_half, cols] + dst[...].astype(F32))
            exchange.start()

        return send, begin

    send_second, begin_second_half = half_exchange(0, slice(0, width), second_w)
    send_second()

    copy_s = to_partner(spreads.at[0], spreads.at[1], 6)
    copy_s.start()

    def begin_second_small():
        place = 0
        for m in range(0, members, 2):
            put(second_s.buf, place, jnp.concatenate([head_grads[m], head_grads[m + 1]], axis=0))
            place += across
        for i in range(3):
            put(second_s.buf, place, wide_rows[i, 1])
            place += across
        clear(second_s.buf, place)
        second_s.start()

    def begin_misc():
        copy_s.wait()
        spread = (spreads[0, 0:1] + spreads[1, 0:1]) * (1.0 / total_members)
        variance = jnp.sum(row_weight * spread, axis=1, keepdims=True)
        misc[...] = jnp.where(
            spot == members, loss, jnp.where(spot == members + 1, variance, misc[...])
        )
        if inner:

            def tell(k, carry):
                second_s.send(misc, misc_out.at[me], 4, mem, lax.rem(me + k, n_rows))
                return carry

            lax.fori_loop(1, n_rows, tell, 0, unroll=True)
            misc_out[me] = misc[...]
        else:
            misc_out[0] = misc[...]

    def begin_second_wide():
        begin_misc()
        begin_second_half()
        grad_w[...] = jnp.zeros_like(grad_w)

    def at(m, steps):
        for when, step in steps:
            pl.when(m == when)(step)

    def each(name, *exchanges):
        def step():
            for exchange in exchanges:
                getattr(exchange, name)()

        return step

    def back_units(m, slot):
        col = once(lambda: column(0.5 * adapter(1, 1, m)))

        def prepare():
            return member_matrix(mats_t[1], col(), adapter(0, 1, m))

        def finish(product):
            grad = product.astype(BF16) * slope(slots[slot], act1[m])
            act1[m] = grad
            return grad

        return finish(contract(keep1[m], prepare(), 1, 0))

    begin_second_small()

    def back_first(i, carry):
        m = 2 * i
        for k in range(2):
            fetch_rise(m + k).wait()

        @pl.when(i < members // 2 - SLOTS // 2)
        def _():
            for k in range(2):
                fetch_rise(m + SLOTS + k).start()

        at(i, back_steps)
        for k in range(2):
            back_units(m + k, lax.rem(m, 2 * SLOTS) + k)
        return carry

    nearly = inner > 1
    back_steps = [(2, begin_second_wide)]
    if nearly:
        back_steps += [(4, second_s.add_near), (6, second_w.add_near)]
    lax.fori_loop(0, members // 2, back_first, 0)

    pairs = members // 2
    wide_rows[0, 0] = jnp.zeros((members, width), F32)

    def place_of(unit):
        m = 2 * lax.rem(unit, pairs)
        return m, pl.ds(pl.multiple_of(unit // pairs * half_cols, half_cols), half_cols)

    def multiply(unit, result):
        m, cols = place_of(unit)
        grads = [act1[m + k, :, cols] for k in range(2)]
        low = jnp.concatenate(grads, axis=1)
        fill = jnp.zeros((embed_t.shape[1] - rows, low.shape[1]), BF16)
        result[...] = contract(embed_t[...], jnp.concatenate([low, fill], axis=0), 1, 0)

    def take_apart(unit, result):
        m, cols = place_of(unit)
        for k in range(2):
            row_sum, out_grad = spread_product(
                result[:, k * half_cols : (k + 1) * half_cols],
                mats[0, :, cols],
                column(adapter(0, 0, m + k)),
                0.5 * adapter(1, 0, m + k, cols),
                grad_w.at[:, cols],
            )
            wide_rows[1, 0, pl.ds(m + k, 1), cols] = out_grad
            wide_rows[2, 0, pl.ds(m + k, 1), cols] = 0.5 * result[
                width : width + 1, k * half_cols : (k + 1) * half_cols
            ]
            wide_rows[0, 0, pl.ds(m + k, 1), :] += row_of(row_sum)

    multiply(0, result_b)

    send_low_half, begin_low_half = half_exchange(1, halves[0], block0_x)
    product_steps = [
        (0, second_s.add_far),
        (1, second_w.add_far),
        (pairs // 2, send_low_half),
        (pairs // 2 + 1, begin_low_half),
    ]
    if nearly:
        product_steps += [(3, second_s.spread), (5, second_w.spread)]

    def product_step(i, carry):
        at(i, product_steps)
        multiply(2 * i + 1, result_a)
        take_apart(2 * i, result_b)
        multiply(2 * i + 2, result_b)
        take_apart(2 * i + 1, result_a)
        return carry

    lax.fori_loop(0, pairs - 1, product_step, 0)
    multiply(2 * pairs - 1, result_a)
    take_apart(2 * pairs - 2, result_b)
    take_apart(2 * pairs - 1, result_a)
    send_high, begin_high = half_exchange(2, halves[1], block1_x)
    send_high()
    for i in range(3):
        put(first_x.buf, i * across, wide_rows[i, 0])
    clear(first_x.buf, 3 * across)
    first_x.start()

    def into_embedding(m, cols):
        return member_matrix(
            mats_t[0, :, cols], column(0.5 * adapter(1, 0, m)), adapter(0, 0, m, cols)
        )

    def embedding_pass(side, cols, steps):
        def body(i, carry):
            at(i, steps)
            members_here = [8 * i + k for k in range(8)]
            low = [into_embedding(m, cols) for m in members_here]
            grads = [act1[m] for m in members_here]
            grad_e[side] += contract(
                jnp.concatenate(grads, axis=1), jnp.concatenate(low, axis=0), 1, 0
            )
            return carry

        lax.fori_loop(0, members // 8, body, 0)

    embedding_pass(0, their_cols, [(1, begin_high), (1, block0_x.add_far)])
    stage_e = slots.at[0, :, pl.ds(0, own_cols)]
    stage_e[...] = grad_e[0].astype(BF16)
    copy_ge = to_partner(stage_e, pair_e, 14)
    copy_ge.start()
    embedding_pass(1, my_cols, [(1, first_x.add_far), (1, block1_x.add_far)])
    copy_ge.wait()
    grad_own = (grad_e[1] + pair_e[...].astype(F32)).T.astype(BF16)
    table_grad = contract(grad_own, one_hot(), 1, 1)
    for f in range(own_feat):
        block = table_grad[edim * f : edim * (f + 1), bins * f : bins * (f + 1)]
        table_x.buf[f] = jnp.concatenate(
            [block, jnp.zeros((edim, LANES - bins), F32)], axis=1
        ).astype(BF16)
    clear(table_x.buf, own_feat)
    table_x.start()
    table_x.add_far()
    second_s.finish()
    second_w.finish()
    if inner:
        part = misc_out.at[pl.ds(0, n_rows - 1)]
        for side in range(2):
            pltpu.make_async_copy(part, part, sems.at[second_s.first + 8 + side]).wait()
    table_x.finish()
    block0_x.finish()
    first_x.finish()
    block1_x.finish()


def adamw(value, grad, first, second, rate):
    first_new = DECAY_FIRST * first + (1.0 - DECAY_FIRST) * grad
    second_new = DECAY_SECOND * second + (1.0 - DECAY_SECOND) * grad * grad
    first_hat = first_new / (1.0 - DECAY_FIRST**STEP)
    second_hat = second_new / (1.0 - DECAY_SECOND**STEP)
    value_new = value - rate * (first_hat / (jnp.sqrt(second_hat) + EPSILON) + WEIGHT_DECAY * value)
    return value_new, first_new, second_new


def update_kernel(*refs):
    count = 23
    ins, outs = refs[:count], refs[count : count + 18]
    held = refs[count + 18 : count + 18 + count]
    made = refs[count + 18 + count : count + 18 + count + 18]
    grad_ref, in_sems, out_sems = refs[-3:]
    copies = [
        pltpu.make_async_copy(src, dst, in_sems.at[i])
        for i, (src, dst) in enumerate(zip(ins, held))
    ]
    for copy in copies:
        copy.start()

    def get(i):
        copies[i].wait()
        return held[i]

    stores = []

    def send(i):
        store = pltpu.make_async_copy(made[i], outs[i], out_sems.at[i])
        store.start()
        stores.append(store)

    mem = lax.axis_index("mem")
    wide = get(0)
    width = grad_ref.shape[0]
    across = width // LANES
    half = width // 2
    tiles = half // TILE * across
    for c in range(2):
        for i in range(half // TILE):
            for j in range(across):
                split = j // 2 * tiles + c * tiles // 2 + i * 2 + j % 2
                whole = c * tiles + i * across + j
                grad_ref[
                    c * half + i * TILE : c * half + (i + 1) * TILE, j * LANES : (j + 1) * LANES
                ] = wide[jnp.where(mem == 0, split, whole)]
    low = grad_ref[...]
    moment = get(1)
    moment_new = MOMENTUM * moment[...] + low.astype(F32)
    made[6][...] = moment_new
    send(6)
    root_l = get(2)
    left = contract(root_l[...].astype(BF16), moment_new.astype(BF16), 1, 0)
    root_r = get(3)
    direction = contract(left.astype(BF16), root_r[...].astype(BF16), 1, 0)
    matrix = get(4)
    made[5][...] = matrix[...] - LR_SHAMPOO * direction
    send(5)
    stat_l = get(5)
    made[7][...] = DECAY_STAT * stat_l[...] + contract(low, low, 1, 1)
    send(7)
    stat_r = get(6)
    made[8][...] = DECAY_STAT * stat_r[...] + contract(low, low, 0, 0)
    send(8)

    def apply(group, news, index, grad, rate):
        results = adamw(group[0][index], grad, group[1][index], group[2][index], rate)
        for new, result in zip(news, results):
            new[index] = result

    second, first, table_grad, misc = [get(i) for i in range(7, 11)]
    adapt = [get(i) for i in range(11, 14)]
    members = adapt[0].shape[2]
    head_tiles = members // 2 * across
    for l, (tiles_ref, place) in enumerate(((first, 0), (second, head_tiles))):
        for i in range(3):
            for j in range(across):
                where = (i, l, slice(None), pl.ds(j * LANES, LANES))
                grad = tiles_ref[place + i * across + j].astype(F32)
                apply(adapt, made[9:12], where, grad, LR_ADAPTER)
    for i in range(9, 12):
        send(i)
    head = [get(i) for i in range(14, 17)]
    classes = head[0].shape[1]
    for m in range(0, members, 2):
        for j in range(across):
            pair = second[m // 2 * across + j].astype(F32)
            for k in range(2):
                where = (m + k, slice(None), pl.ds(j * LANES, LANES))
                part = pair[k * classes : (k + 1) * classes]
                apply(head, made[12:15], where, part, LR_HEAD)
    for i in range(12, 15):
        send(i)
    table = [get(i) for i in range(17, 20)]
    own_feat, bins = table[0].shape[0], table[0].shape[2]
    for f in range(own_feat):
        apply(table, made[2:5], f, table_grad[f][:, :bins].astype(F32), LR_TABLE)
    for i in range(2, 5):
        send(i)
    bias = [get(i) for i in range(20, 23)]
    total = misc[0]
    for k in range(1, misc.shape[0]):
        total = total + misc[k]
    apply(bias, made[15:18], Ellipsis, total[:, :members], LR_BIAS)
    made[0][...] = jnp.broadcast_to(total[0:1, members : members + 1], made[0].shape)
    made[1][...] = jnp.broadcast_to(total[0:1, members + 1 : members + 2], made[1].shape)
    for i in (0, 1, 15, 16, 17):
        send(i)
    for store in stores:
        store.wait()


def shards(
    n_rows,
    bin_index,
    labels,
    row_weight,
    bin_table,
    table_first,
    table_second,
    weights,
    weights_moment,
    stat_left,
    stat_right,
    root_left,
    root_right,
    adapters,
    adapter_first,
    adapter_second,
    head_weight,
    head_first,
    head_second,
    head_bias,
    bias_first,
    bias_second,
):
    rows = bin_index.shape[0]
    width = weights.shape[2]
    members, _, classes = head_weight.shape
    own_feat = bin_table.shape[0]
    across = width // LANES
    half_tiles = width // 2 // TILE * across
    head_tiles = members // 2 * across
    inner = 0 if SHARES % n_rows else INNER
    fit = lambda count: -(-count // SHARES) * SHARES
    sizes = (
        (inner, half_tiles),
        (inner, fit(head_tiles + 3 * across)),
        (1, fit(own_feat)),
        (1, half_tiles // 2),
        (1, half_tiles // 2),
        (1, fit(3 * across)),
    )

    def tiles(*shape, kind=BF16):
        return pltpu.VMEM((*shape, TILE, LANES), kind)

    stages = []
    for i, (near, count) in enumerate(sizes):
        if inner:
            far = n_rows // near
            block = count // near
            kind = F32 if near > 1 else BF16
            stages += [
                tiles(count),
                tiles(max(near - 1, 1), block if near > 1 else 1),
                tiles(block if near > 1 else 1, kind=kind),
                tiles(far - 1, block // far, kind=kind),
                tiles(count, kind=F32 if i == 1 else BF16),
            ]
        else:
            stages += [tiles(count)] + [tiles(1)] * 4
    tables = [jnp.swapaxes(x, 1, 2) for x in (bin_table, table_first, table_second)]
    heads = [jnp.swapaxes(x, 1, 2) for x in (head_weight, head_first, head_second)]
    biases = [jnp.transpose(x) for x in (head_bias, bias_first, bias_second)]
    squares = [x[0] for x in (weights, weights_moment, stat_left, stat_right, root_left, root_right)]
    in_vmem = pl.BlockSpec(memory_space=pltpu.VMEM)
    in_hbm = pl.BlockSpec(memory_space=pl.ANY)
    struct = jax.ShapeDtypeStruct
    grad_tiles = lambda count: struct((count, TILE, LANES), BF16)
    big = pltpu.VMEM((members, rows, width), BF16)
    wide, second, first, table, misc, _, _ = pl.pallas_call(
        functools.partial(step_kernel, n_rows, inner),
        out_shape=(
            grad_tiles(2 * half_tiles),
            struct((sizes[1][1], TILE, LANES), F32),
            grad_tiles(sizes[5][1]),
            grad_tiles(sizes[2][1]),
            struct((n_rows if inner else 1, classes, LANES), F32),
            struct((members, rows, width), BF16),
            struct((members, rows, width), BF16),
        ),
        in_specs=[in_vmem] * 4 + [in_hbm] + [in_vmem] * 3,
        out_specs=(in_vmem,) * 5 + (in_hbm,) * 2,
        scratch_shapes=[
            pltpu.VMEM((rows, width), BF16),
            pltpu.VMEM((2, width, width), F32),
            pltpu.VMEM((2, width, width), BF16),
            big,
            big,
            pltpu.VMEM((members, classes, rows), F32),
            pltpu.VMEM((2 * SLOTS, rows, width), BF16),
            pltpu.VMEM((width + TILE, -(-rows // LANES) * LANES), BF16),
            pltpu.VMEM((3 * width // 2, width), BF16),
            pltpu.VMEM((2, rows, width // 2), F32),
            pltpu.VMEM((width, width), F32),
            pltpu.VMEM((2, classes, rows), F32),
            pltpu.VMEM((2, 8, rows), F32),
            pltpu.VMEM((width + TILE, width), F32),
            pltpu.VMEM((width + TILE, width), F32),
            pltpu.VMEM((rows, width // 2), BF16),
            pltpu.VMEM((3 * width // 2, width), BF16),
            pltpu.VMEM((3, 2, members, width), F32),
            pltpu.VMEM((members, classes, width), F32),
            pltpu.VMEM((classes, LANES), F32),
            pltpu.SemaphoreType.DMA((16 + 6 * EXCHANGE_SEMS,)),
            pltpu.SemaphoreType.DMA((2 * SLOTS,)),
            *stages,
        ],
        compiler_params=pltpu.CompilerParams(
            collective_id=0, has_side_effects=True, vmem_limit_bytes=64 * 2**20
        ),
        name="step",
    )(
        jnp.transpose(bin_index),
        labels[None],
        row_weight[None],
        tables[0],
        squares[0],
        adapters,
        heads[0],
        biases[0],
    )
    if not inner:
        wide, second, first, table, misc = lax.psum(
            (wide.astype(F32), second.astype(F32), first.astype(F32), table.astype(F32), misc),
            "rows",
        )
        first, table = [x.astype(BF16) for x in (first, table)]
        halves = lax.all_gather(wide.astype(BF16), "mem").reshape(2, 2, half_tiles, TILE, LANES)
        parts = halves[:, 0].reshape(2, 2, half_tiles // 2, TILE, LANES)
        wide = jnp.where(
            lax.axis_index("mem") == 0,
            jnp.swapaxes(parts, 0, 1).reshape(-1, TILE, LANES),
            halves[:, 1].reshape(-1, TILE, LANES),
        )
    one = struct((1, LANES), F32)
    like = lambda x: struct(x.shape, F32)
    ins = (
        wide,
        squares[1],
        squares[4],
        squares[5],
        squares[0],
        squares[2],
        squares[3],
        second,
        first,
        table,
        misc,
        adapters,
        adapter_first,
        adapter_second,
        *heads,
        *tables,
        *biases,
    )
    results = (
        one,
        one,
        *[like(x) for x in tables],
        *[like(squares[0])] * 4,
        *[like(adapters)] * 3,
        *[like(x) for x in heads],
        *[like(x) for x in biases],
    )
    outs = pl.pallas_call(
        update_kernel,
        out_shape=results,
        in_specs=[in_hbm] * len(ins),
        out_specs=(in_hbm,) * len(results),
        scratch_shapes=[pltpu.VMEM(x.shape, x.dtype) for x in ins]
        + [pltpu.VMEM(x.shape, x.dtype) for x in results]
        + [
            pltpu.VMEM((width, width), BF16),
            pltpu.SemaphoreType.DMA((len(ins),)),
            pltpu.SemaphoreType.DMA((len(results),)),
        ],
        compiler_params=pltpu.CompilerParams(vmem_limit_bytes=60 * 2**20),
        name="update",
    )(*ins)
    back = lambda xs: [jnp.swapaxes(x, 1, 2) for x in xs]
    return (
        outs[0][0, 0],
        outs[1][0, 0],
        *back(outs[2:5]),
        *[x[None] for x in outs[5:9]],
        *outs[9:12],
        *back(outs[12:15]),
        *[jnp.transpose(x) for x in outs[15:18]],
    )


def solution(mesh):
    tables = P("mem", None, None)
    adapt = P(None, None, "mem", None)
    pair = P("mem", None)
    return jax.shard_map(
        functools.partial(shards, mesh.shape["rows"]),
        mesh=mesh,
        in_specs=(P("rows", "mem"), P("rows"), P("rows"))
        + (tables,) * 9
        + (adapt,) * 3
        + (tables,) * 3
        + (pair,) * 3,
        out_specs=(P(), P()) + (tables,) * 7 + (adapt,) * 3 + (tables,) * 3 + (pair,) * 3,
        check_vma=False,
    )
```
